32 devices in a mesh: groups: 2 (over y), context: 4 (over z), tensor: 4 (over x, core).
Axes of the slice: x: 2, y: 2, z: 4, core: 2. Of those that a mesh axis runs over, the one named last changes fastest.
Arguments:
- outer_gate: bfloat16 [1024, 8192], P(('groups', 'context'), 'tensor'), parts along dimension 0, may hold values from -6 to 6
- inner_gate: bfloat16 [1024, 8192], P(('groups', 'context'), 'tensor'), parts along dimension 0, may hold values from -6 to 6
- value_path: bfloat16 [1024, 8192], P(('groups', 'context'), 'tensor'), parts along dimension 0, may hold values from -6 to 6
- long_filter: bfloat16 [512, 8192], P('context', 'tensor'), may hold values from -0.25 to 0.25
- skip_scale: float32 [8192], P('tensor'), may hold values from 0.5 to 1.5
- out_weight: bfloat16 [8192, 8192], P('context'), may hold values from -0.0625 to 0.0625
Outputs:
- projected: bfloat16 [1024, 8192], P(('groups', 'context'), 'tensor'), parts along dimension 0
The draws below stay inside these ranges and needn't reach their ends.
There are 2 independent parts, one for each index of `groups`. The reference program is written for one: setup_inputs(seed, part) draws one part's arguments, and reference() takes and returns one part's arrays. A program takes and returns all parts, laid end to end along the dimension named above; an argument that names none is the same for every part. Nothing has to cross between parts.
All inputs are finite; a program needn't handle non-finite values.
Results may differ from the reference program's by a relative error of at most 0.005.
Values may be sent and summed in bfloat16 or wider, within the bound.
A program may use at most 192 MiB of HBM per device.

```python
import jax
import jax.numpy as jnp
from jax import lax

D = 8192
LENGTH = 512


def levels(key, extent, pieces, least, top_value):
    def one(position, parts):
        steps = jax.random.uniform(jax.random.fold_in(jax.random.fold_in(key, 6), position), (parts,), jnp.float32, least / len(pieces), top_value / len(pieces))
        return jnp.repeat(jnp.exp(steps), extent[position] // parts).reshape((-1,) + (1,) * (len(extent) - position - 1))

    loudness = one(*pieces[0])
    for cut in pieces[1:]:
        loudness = loudness * one(*cut)
    return loudness


def normal_values(stream_key, dims, deviation, bound, pieces=(), held_as=jnp.bfloat16):
    array = jax.random.normal(stream_key, dims, jnp.float32) * deviation
    if len(pieces) > 0:
        array = levels(stream_key, dims, pieces, -0.22, 0.18) * array
    return jnp.clip(array, min=-bound, max=bound).astype(held_as)


def setup_inputs(seed: int = 0, part: int = 0) -> dict:
    splits = jax.random.split(jax.random.key(seed), 7)
    own_keys = jax.random.split(jax.random.fold_in(splits[6], part), 7)
    outer_gate = normal_values(own_keys[0], (LENGTH, D), 1.0, 6.0, ((0, 4), (1, 4)))
    inner_gate = normal_values(own_keys[1], (LENGTH, D), 1.0, 6.0, ((0, 4), (1, 4)))
    value_path = normal_values(own_keys[2], (LENGTH, D), 1.0, 6.0, ((0, 4), (1, 4)))
    long_filter = normal_values(splits[3], (LENGTH, D), LENGTH ** -0.5, 0.25, ((0, 4), (1, 4)))
    skip_scale = jnp.clip(0.5 + 1.0 * jax.random.uniform(splits[4], (D,), jnp.float32) ** levels(splits[4], (D,), ((0, 4),), -0.2, 0.2), 0.5, 1.5)
    out_weight = normal_values(splits[5], (D, D), D ** -0.5, 0.0625, ((0, 4),))
    return {"outer_gate": outer_gate, "inner_gate": inner_gate, "value_path": value_path, "long_filter": long_filter, "skip_scale": skip_scale, "out_weight": out_weight}


def convolve(pair):
    signal_block, filter_block = pair
    length = signal_block.shape[0]
    padded_len = 2 * length
    signal_spec = jnp.fft.rfft(signal_block, n=padded_len, axis=0)
    filter_spec = jnp.fft.rfft(filter_block, n=padded_len, axis=0)
    return jnp.fft.irfft(signal_spec * filter_spec, n=padded_len, axis=0)[:length]


def reference(outer_gate, inner_gate, value_path, long_filter, skip_scale, out_weight):
    length, model_width = inner_gate.shape
    mixed_in = inner_gate.astype(jnp.float32) * value_path.astype(jnp.float32)
    filter_full = long_filter.astype(jnp.float32)
    group_count = model_width // 128
    signal_blocks = mixed_in.reshape(length, group_count, 128).transpose(1, 0, 2)
    filter_blocks = filter_full.reshape(length, group_count, 128).transpose(1, 0, 2)
    conv_blocks = lax.map(convolve, (signal_blocks, filter_blocks))
    conv = conv_blocks.transpose(1, 0, 2).reshape(length, model_width).astype(jnp.float32)
    gated = (outer_gate.astype(jnp.float32) * (conv + skip_scale[None, :] * mixed_in)).astype(jnp.bfloat16)
    return jnp.dot(gated, out_weight, preferred_element_type=jnp.float32).astype(jnp.bfloat16)
```

```python
import math

import jax
import jax.numpy as jnp
import ml_dtypes
import numpy as np
from jax import lax
from jax.sharding import PartitionSpec as P


def transform_tables(length):
    index = np.arange(length, dtype=np.int64)
    turns = ((4 * index[:, None] + 1) * index[None, :]) % (4 * length)
    angle = turns * (2.0 * math.pi / (4 * length))
    table = np.concatenate([np.cos(angle), -np.sin(angle)], axis=0)
    high = table.astype(ml_dtypes.bfloat16)
    low = (table - high.astype(np.float64)).astype(ml_dtypes.bfloat16)
    return high, low


def mm(a, b):
    return jnp.dot(a, b, preferred_element_type=jnp.float32)


def causal_conv(high, low, high_t, low_t, signal, kernel):
    length = signal.shape[0]
    spec_s = mm(high, signal) + mm(low, signal)
    spec_k = mm(high, kernel) + mm(low, kernel)
    s_re, s_im = spec_s[:length], spec_s[length:]
    k_re, k_im = spec_k[:length], spec_k[length:]
    prod = jnp.concatenate([s_re * k_re - s_im * k_im, s_re * k_im + s_im * k_re], axis=0)
    p_high = prod.astype(jnp.bfloat16)
    p_low = (prod - p_high.astype(jnp.float32)).astype(jnp.bfloat16)
    return (mm(high_t, p_high) + mm(low_t, p_high) + mm(high_t, p_low)) * (1.0 / length)


def body(outer_gate, inner_gate, value_path, long_filter, skip_scale, out_weight):
    n_ctx = lax.axis_size("context")
    n_ten = lax.axis_size("tensor")
    ctx = lax.axis_index("context")
    ten = lax.axis_index("tensor")
    positions, width = inner_gate.shape
    sub = width // n_ctx
    length = n_ctx * positions
    high, low = transform_tables(length)
    mixed = (inner_gate.astype(jnp.float32) * value_path.astype(jnp.float32)).astype(jnp.bfloat16)
    stacked = jnp.stack([mixed, outer_gate, long_filter])
    stacked = lax.all_to_all(stacked, "context", split_axis=2, concat_axis=1, tiled=True)
    signal, outer, kernel = stacked[0], stacked[1], stacked[2]
    conv = causal_conv(high, low, np.ascontiguousarray(high.T), np.ascontiguousarray(low.T), signal, kernel)
    skip = lax.dynamic_slice_in_dim(skip_scale, ctx * sub, sub, 0)
    gated = (
        outer.astype(jnp.float32) * (conv + skip[None, :] * signal.astype(jnp.float32))
    ).astype(jnp.bfloat16)
    pairs = [(c * n_ten + t, t * n_ctx + c) for c in range(n_ctx) for t in range(n_ten)]
    gated = lax.ppermute(gated, ("context", "tensor"), pairs)
    features = lax.all_gather(gated, "tensor", axis=1, tiled=True)
    columns = out_weight.shape[1] // n_ten
    own = lax.dynamic_slice_in_dim(out_weight, ten * columns, columns, 1)
    partial = mm(features, own).astype(jnp.bfloat16).reshape(n_ctx, positions, columns)
    partial = lax.all_to_all(partial, "context", split_axis=0, concat_axis=0, tiled=True)
    return jnp.sum(partial.astype(jnp.float32), axis=0).astype(jnp.bfloat16)


def solution(mesh):
    placed = (
        P(("groups", "context"), "tensor"),
        P(("groups", "context"), "tensor"),
        P(("groups", "context"), "tensor"),
        P("context", "tensor"),
        P("tensor"),
        P("context", None),
    )
    return jax.shard_map(
        body,
        mesh=mesh,
        in_specs=placed,
        out_specs=P(("groups", "context"), "tensor"),
        check_vma=False,
    )
```

```python
import functools
import math

import jax
import jax.numpy as jnp
import ml_dtypes
import numpy as np
from jax import lax
from jax.experimental import pallas as pl
from jax.experimental.pallas import tpu as pltpu
from jax.sharding import PartitionSpec as P


def transform_tables(length):
    index = np.arange(length, dtype=np.int64)
    turns = ((4 * index[:, None] + 1) * index[None, :]) % (4 * length)
    angle = turns * (2.0 * math.pi / (4 * length))
    table = np.concatenate([np.cos(angle), -np.sin(angle)], axis=0)
    high = table.astype(ml_dtypes.bfloat16)
    low = (table - high.astype(np.float64)).astype(ml_dtypes.bfloat16)
    return high, low


def mm(a, b):
    return jnp.dot(a, b, preferred_element_type=jnp.float32)


def causal_conv(high, low, high_t, low_t, signal, kernel):
    length = signal.shape[0]
    spec_s = mm(high, signal) + mm(low, signal)
    spec_k = mm(high, kernel) + mm(low, kernel)
    s_re, s_im = spec_s[:length], spec_s[length:]
    k_re, k_im = spec_k[:length], spec_k[length:]
    prod = jnp.concatenate([s_re * k_re - s_im * k_im, s_re * k_im + s_im * k_re], axis=0)
    p_high = prod.astype(jnp.bfloat16)
    p_low = (prod - p_high.astype(jnp.float32)).astype(jnp.bfloat16)
    return (mm(high_t, p_high) + mm(low_t, p_high) + mm(high_t, p_low)) * (1.0 / length)


def body_plain(outer_gate, inner_gate, value_path, long_filter, skip_scale, out_weight):
    n_ctx = lax.axis_size("context")
    n_ten = lax.axis_size("tensor")
    ctx = lax.axis_index("context")
    ten = lax.axis_index("tensor")
    positions, width = inner_gate.shape
    sub = width // n_ctx
    length = n_ctx * positions
    high, low = transform_tables(length)
    mixed = (inner_gate.astype(jnp.float32) * value_path.astype(jnp.float32)).astype(jnp.bfloat16)
    stacked = jnp.stack([mixed, outer_gate, long_filter])
    stacked = lax.all_to_all(stacked, "context", split_axis=2, concat_axis=1, tiled=True)
    signal, outer, kernel = stacked[0], stacked[1], stacked[2]
    conv = causal_conv(high, low, np.ascontiguousarray(high.T), np.ascontiguousarray(low.T), signal, kernel)
    skip = lax.dynamic_slice_in_dim(skip_scale, ctx * sub, sub, 0)
    gated = (
        outer.astype(jnp.float32) * (conv + skip[None, :] * signal.astype(jnp.float32))
    ).astype(jnp.bfloat16)
    pairs = [(c * n_ten + t, t * n_ctx + c) for c in range(n_ctx) for t in range(n_ten)]
    gated = lax.ppermute(gated, ("context", "tensor"), pairs)
    features = lax.all_gather(gated, "tensor", axis=1, tiled=True)
    columns = out_weight.shape[1] // n_ten
    own = lax.dynamic_slice_in_dim(out_weight, ten * columns, columns, 1)
    partial = mm(features, own).astype(jnp.bfloat16).reshape(n_ctx, positions, columns)
    partial = lax.all_to_all(partial, "context", split_axis=0, concat_axis=0, tiled=True)
    return jnp.sum(partial.astype(jnp.float32), axis=0).astype(jnp.bfloat16)


MESH = pl.DeviceIdType.MESH
PARTS = 2
BLOCK = 128
TILE = 256


def blocked_tables(length):
    high, low = transform_tables(length)

    def order(table):
        halves = table.reshape(2, length // BLOCK, BLOCK, length)
        return np.ascontiguousarray(halves.transpose(1, 0, 2, 3).reshape(2 * length, length))

    high, low = order(high), order(low)
    return high, low, np.ascontiguousarray(high.T), np.ascontiguousarray(low.T)


def fused(
    n_ctx, n_ten,
    outer_ref, inner_ref, value_ref, filter_ref, skip_ref, w_hbm, fh_hbm, fl_hbm, gh_hbm, gl_hbm,
    out_ref,
    w, fh, fl, gh, gl, stage, rx, skip_stage, skip_rx, acc, feats, pbuf, rbuf, own,
    load_sem, send1, recv1, send_skip, recv_skip, send2, recv2, send3, recv3,
):
    ctx = lax.axis_index("context")
    ten = lax.axis_index("tensor")
    grp = lax.axis_index("groups")
    me = ctx * n_ten + ten
    total = n_ctx * n_ten
    positions, width = inner_ref.shape
    sub = width // n_ctx
    part = sub // PARTS
    length = n_ctx * positions
    columns = w.shape[1]

    loads = [
        pltpu.make_async_copy(a, b, load_sem.at[i])
        for i, (a, b) in enumerate(
            [
                (fh_hbm, fh), (fl_hbm, fl), (gh_hbm, gh), (gl_hbm, gl),
                (w_hbm.at[:, pl.ds(pl.multiple_of(ten * columns, 128), columns)], w),
            ]
        )
    ]
    for load in loads:
        load.start()

    barrier = pltpu.get_barrier_semaphore()
    for d in range(1, total):
        other = lax.rem(me + d, total)
        pl.semaphore_signal(
            barrier, inc=1, device_id=(grp, other // n_ten, lax.rem(other, n_ten)), device_id_type=MESH
        )
    stage[0] = (inner_ref[...].astype(jnp.float32) * value_ref[...].astype(jnp.float32)).astype(jnp.bfloat16)
    stage[1] = outer_ref[...]
    stage[2] = filter_ref[...]
    skip_stage[...] = jnp.broadcast_to(skip_ref[...], skip_stage.shape)
    pl.semaphore_wait(barrier, total - 1)

    def input_copies(j):
        unit = ten * n_ctx + j
        to = (grp, unit // n_ten, lax.rem(unit, n_ten))
        pieces = []
        for h in range(PARTS):
            pieces.append((
                stage.at[:, :, pl.ds(j * sub + h * part, part)],
                rx.at[h, :, pl.ds(pl.multiple_of(ctx * positions, positions), positions), :],
                send1.at[h, j], recv1.at[h, ctx],
            ))
        pieces.append((
            skip_stage.at[:, pl.ds(j * sub, sub)], skip_rx.at[ctx], send_skip.at[j], recv_skip.at[ctx],
        ))
        return unit, to, pieces

    def remote(piece, to):
        a, b, s, r = piece
        return pltpu.make_async_remote_copy(
            src_ref=a, dst_ref=b, send_sem=s, recv_sem=r, device_id=to, device_id_type=MESH
        )

    for i in [PARTS] + list(range(PARTS)):
        for j in range(n_ctx):
            unit, to, pieces = input_copies(j)

            @pl.when(unit != me)
            def _():
                remote(pieces[i], to).start()

            @pl.when(unit == me)
            def _():
                a, b, s, r = pieces[i]
                pltpu.make_async_copy(a, b, r).start()

    for load in loads[:4]:
        load.wait()

    def landed(ref, sem):
        pltpu.make_async_copy(ref, ref, sem).wait()

    for p in range(n_ctx):
        landed(skip_rx.at[p], recv_skip.at[p])

    def gather_copy(h, k):
        here = feats.at[:, pl.ds(pl.multiple_of(ten * sub + h * part, 128), part)]
        return pltpu.make_async_remote_copy(
            src_ref=here, dst_ref=here, send_sem=send2.at[h, k], recv_sem=recv2.at[h, k],
            device_id=(grp, ctx, lax.rem(ten + k, n_ten)), device_id_type=MESH,
        )

    for h in range(PARTS):
        for p in range(n_ctx):
            landed(rx.at[h, :, pl.ds(p * positions, positions), :], recv1.at[h, p])
        acc[...] = jnp.zeros_like(acc)

        @pl.loop(0, length // BLOCK)
        def _(b):
            rows = pl.ds(pl.multiple_of(b * 2 * BLOCK, 2 * BLOCK), 2 * BLOCK)
            f_high, f_low = fh[rows, :], fl[rows, :]
            signal, kernel = rx[h, 0], rx[h, 2]
            spec_s = mm(f_high, signal) + mm(f_low, signal)
            spec_k = mm(f_high, kernel) + mm(f_low, kernel)
            s_re, s_im = spec_s[:BLOCK], spec_s[BLOCK:]
            k_re, k_im = spec_k[:BLOCK], spec_k[BLOCK:]
            prod = jnp.concatenate([s_re * k_re - s_im * k_im, s_re * k_im + s_im * k_re], axis=0)
            p_high = prod.astype(jnp.bfloat16)
            p_low = (prod - p_high.astype(jnp.float32)).astype(jnp.bfloat16)
            g_high, g_low = gh[:, rows], gl[:, rows]
            acc[...] += mm(g_high, p_high) + mm(g_low, p_high) + mm(g_high, p_low)

        skip = skip_rx[0, 0:1, h * part:(h + 1) * part]
        gated = rx[h, 1].astype(jnp.float32) * (
            acc[...] * (1.0 / length) + skip * rx[h, 0].astype(jnp.float32)
        )
        feats[:, pl.ds(pl.multiple_of(ten * sub + h * part, 128), part)] = gated.astype(jnp.bfloat16)
        for k in range(1, n_ten):
            gather_copy(h, k).start()

    loads[4].wait()
    for h in range(PARTS):
        for k in range(1, n_ten):
            came = lax.rem(ten + n_ten - k, n_ten)
            landed(feats.at[:, pl.ds(pl.multiple_of(came * sub + h * part, 128), part)], recv2.at[h, k])

    def partial_copy(k):
        return pltpu.make_async_remote_copy(
            src_ref=pbuf.at[k], dst_ref=rbuf.at[k], send_sem=send3.at[k], recv_sem=recv3.at[k],
            device_id=(grp, lax.rem(ctx + k, n_ctx), ten), device_id_type=MESH,
        )

    order = sorted(range(1, n_ctx), key=lambda k: abs(k - n_ctx / 2))
    for k in order + [0]:
        q = lax.rem(ctx + k, n_ctx)
        rows = pl.ds(pl.multiple_of(q * positions, positions), positions)

        @pl.loop(0, columns // TILE)
        def _(n):
            cols = pl.ds(pl.multiple_of(n * TILE, TILE), TILE)
            product = mm(feats[rows, :], w[:, cols])
            if k == 0:
                own[:, cols] = product
            else:
                pbuf[k, :, cols] = product.astype(jnp.bfloat16)

        if k:
            partial_copy(k).start()

    result = own[...]
    for k in order:
        landed(rbuf.at[k], recv3.at[k])
        result = result + rbuf[k].astype(jnp.float32)
    out_ref[...] = result.astype(jnp.bfloat16)

    for i in range(PARTS + 1):
        for j in range(n_ctx):
            unit, to, pieces = input_copies(j)

            @pl.when(unit != me)
            def _():
                remote(pieces[i], to).wait_send()
    for h in range(PARTS):
        for k in range(1, n_ten):
            gather_copy(h, k).wait_send()
    for k in order:
        partial_copy(k).wait_send()


def body(outer_gate, inner_gate, value_path, long_filter, skip_scale, out_weight):
    n_ctx = lax.axis_size("context")
    n_ten = lax.axis_size("tensor")
    positions, width = inner_gate.shape
    sub = width // n_ctx
    length = n_ctx * positions
    columns = out_weight.shape[1] // n_ten
    if sub % (PARTS * 128) or length % BLOCK or columns % TILE or positions % 16 or length > 1024:
        return body_plain(outer_gate, inner_gate, value_path, long_filter, skip_scale, out_weight)
    tables = [jnp.asarray(t) for t in blocked_tables(length)]
    bf16, f32 = jnp.bfloat16, jnp.float32
    part = sub // PARTS
    dma = pltpu.SemaphoreType.DMA
    vmem = pl.BlockSpec(memory_space=pltpu.VMEM)
    hbm = pl.BlockSpec(memory_space=pl.ANY)
    return pl.pallas_call(
        functools.partial(fused, n_ctx, n_ten),
        out_shape=jax.ShapeDtypeStruct((positions, columns), bf16),
        in_specs=[vmem] * 5 + [hbm] * 5,
        out_specs=vmem,
        scratch_shapes=[
            pltpu.VMEM((out_weight.shape[0], columns), bf16),
            pltpu.VMEM((2 * length, length), bf16),
            pltpu.VMEM((2 * length, length), bf16),
            pltpu.VMEM((length, 2 * length), bf16),
            pltpu.VMEM((length, 2 * length), bf16),
            pltpu.VMEM((3, positions, width), bf16),
            pltpu.VMEM((PARTS, 3, length, part), bf16),
            pltpu.VMEM((8, width), f32),
            pltpu.VMEM((n_ctx, 8, sub), f32),
            pltpu.VMEM((length, part), f32),
            pltpu.VMEM((length, n_ten * sub), bf16),
            pltpu.VMEM((n_ctx, positions, columns), bf16),
            pltpu.VMEM((n_ctx, positions, columns), bf16),
            pltpu.VMEM((positions, columns), f32),
            dma((5,)),
            dma((PARTS, n_ctx)), dma((PARTS, n_ctx)),
            dma((n_ctx,)), dma((n_ctx,)),
            dma((PARTS, n_ten)), dma((PARTS, n_ten)),
            dma((n_ctx,)), dma((n_ctx,)),
        ],
        compiler_params=pltpu.CompilerParams(
            collective_id=0, has_side_effects=True, vmem_limit_bytes=56 * 1024 * 1024
        ),
    )(outer_gate, inner_gate, value_path, long_filter, skip_scale[None, :], out_weight, *tables)


def solution(mesh):
    placed = (
        P(("groups", "context"), "tensor"),
        P(("groups", "context"), "tensor"),
        P(("groups", "context"), "tensor"),
        P("context", "tensor"),
        P("tensor"),
        P("context", None),
    )
    return jax.shard_map(
        body,
        mesh=mesh,
        in_specs=placed,
        out_specs=P(("groups", "context"), "tensor"),
        check_vma=False,
    )
```

```python
import functools
import math

import jax
import jax.numpy as jnp
import ml_dtypes
import numpy as np
from jax import lax
from jax.experimental import pallas as pl
from jax.experimental.pallas import tpu as pltpu
from jax.sharding import PartitionSpec as P


def transform_tables(length):
    index = np.arange(length, dtype=np.int64)
    turns = ((4 * index[:, None] + 1) * index[None, :]) % (4 * length)
    angle = turns * (2.0 * math.pi / (4 * length))
    table = np.concatenate([np.cos(angle), -np.sin(angle)], axis=0)
    high = table.astype(ml_dtypes.bfloat16)
    low = (table - high.astype(np.float64)).astype(ml_dtypes.bfloat16)
    return high, low


def mm(a, b):
    return jnp.dot(a, b, preferred_element_type=jnp.float32)


def causal_conv(high, low, high_t, low_t, signal, kernel):
    length = signal.shape[0]
    spec_s = mm(high, signal) + mm(low, signal)
    spec_k = mm(high, kernel) + mm(low, kernel)
    s_re, s_im = spec_s[:length], spec_s[length:]
    k_re, k_im = spec_k[:length], spec_k[length:]
    prod = jnp.concatenate([s_re * k_re - s_im * k_im, s_re * k_im + s_im * k_re], axis=0)
    p_high = prod.astype(jnp.bfloat16)
    p_low = (prod - p_high.astype(jnp.float32)).astype(jnp.bfloat16)
    return (mm(high_t, p_high) + mm(low_t, p_high) + mm(high_t, p_low)) * (1.0 / length)


def body_plain(outer_gate, inner_gate, value_path, long_filter, skip_scale, out_weight):
    n_ctx = lax.axis_size("context")
    n_ten = lax.axis_size("tensor")
    ctx = lax.axis_index("context")
    ten = lax.axis_index("tensor")
    positions, width = inner_gate.shape
    sub = width // n_ctx
    length = n_ctx * positions
    high, low = transform_tables(length)
    mixed = (inner_gate.astype(jnp.float32) * value_path.astype(jnp.float32)).astype(jnp.bfloat16)
    stacked = jnp.stack([mixed, outer_gate, long_filter])
    stacked = lax.all_to_all(stacked, "context", split_axis=2, concat_axis=1, tiled=True)
    signal, outer, kernel = stacked[0], stacked[1], stacked[2]
    conv = causal_conv(high, low, np.ascontiguousarray(high.T), np.ascontiguousarray(low.T), signal, kernel)
    skip = lax.dynamic_slice_in_dim(skip_scale, ctx * sub, sub, 0)
    gated = (
        outer.astype(jnp.float32) * (conv + skip[None, :] * signal.astype(jnp.float32))
    ).astype(jnp.bfloat16)
    pairs = [(c * n_ten + t, t * n_ctx + c) for c in range(n_ctx) for t in range(n_ten)]
    gated = lax.ppermute(gated, ("context", "tensor"), pairs)
    features = lax.all_gather(gated, "tensor", axis=1, tiled=True)
    columns = out_weight.shape[1] // n_ten
    own = lax.dynamic_slice_in_dim(out_weight, ten * columns, columns, 1)
    partial = mm(features, own).astype(jnp.bfloat16).reshape(n_ctx, positions, columns)
    partial = lax.all_to_all(partial, "context", split_axis=0, concat_axis=0, tiled=True)
    return jnp.sum(partial.astype(jnp.float32), axis=0).astype(jnp.bfloat16)


MESH = pl.DeviceIdType.MESH
PARTS = 2
BLOCK = 128
TILE = 256


def blocked_tables(length):
    high, low = transform_tables(length)

    def order(table):
        halves = table.reshape(2, length // BLOCK, BLOCK, length)
        return np.ascontiguousarray(halves.transpose(1, 0, 2, 3).reshape(2 * length, length))

    high, low = order(high), order(low)
    return high, low, np.ascontiguousarray(high.T), np.ascontiguousarray(low.T)


def fused(
    n_ctx, n_ten,
    outer_ref, inner_ref, value_ref, filter_ref, skip_ref, w_hbm, fh_hbm, fl_hbm, gh_hbm, gl_hbm,
    out_ref,
    w, fh, fl, gh, gl, stage, mid, rx, skip_stage, skip_rx, acc, feats, pbuf, rbuf, own,
    load_sem, send_x, recv_x, send1, recv1, send_skip, recv_skip, send2, recv2, send3, recv3,
):
    ctx = lax.axis_index("context")
    ten = lax.axis_index("tensor")
    grp = lax.axis_index("groups")
    positions, width = inner_ref.shape
    sub = width // n_ctx
    part = sub // PARTS
    length = n_ctx * positions
    columns = w.shape[1]

    loads = [
        pltpu.make_async_copy(a, b, load_sem.at[i])
        for i, (a, b) in enumerate(
            [
                (fh_hbm, fh), (fl_hbm, fl), (gh_hbm, gh), (gl_hbm, gl),
                (w_hbm.at[:, pl.ds(pl.multiple_of(ten * columns, 128), columns)], w),
            ]
        )
    ]
    for load in loads:
        load.start()

    barrier = pltpu.get_barrier_semaphore()
    for k in range(1, n_ten):
        pl.semaphore_signal(
            barrier, inc=1, device_id=(grp, ctx, lax.rem(ten + k, n_ten)), device_id_type=MESH
        )
    for k in range(1, n_ctx):
        pl.semaphore_signal(
            barrier, inc=1, device_id=(grp, lax.rem(ctx + k, n_ctx), ten), device_id_type=MESH
        )
    stage[0] = (inner_ref[...].astype(jnp.float32) * value_ref[...].astype(jnp.float32)).astype(jnp.bfloat16)
    stage[1] = outer_ref[...]
    stage[2] = filter_ref[...]
    skip_stage[...] = jnp.broadcast_to(skip_ref[...], skip_stage.shape)
    pl.semaphore_wait(barrier, n_ten + n_ctx - 2)

    def landed(ref, sem):
        pltpu.make_async_copy(ref, ref, sem).wait()

    def slab(j, h):
        return stage.at[:, :, pl.ds(pl.multiple_of(j * sub + h * part, 128), part)]

    def across(h, k):
        j = lax.rem(ten + k, n_ten)
        return pltpu.make_async_remote_copy(
            src_ref=slab(j, h), dst_ref=mid.at[h, k], send_sem=send_x.at[h, k], recv_sem=recv_x.at[h, k],
            device_id=(grp, ctx, j), device_id_type=MESH,
        )

    def along(h, k):
        return lax.rem(ten + n_ten - k, n_ten), (
            mid.at[h, k] if k else slab(ten, h),
            rx.at[h, :, pl.ds(pl.multiple_of(ctx * positions, positions), positions), :],
            send1.at[h, k], recv1.at[h, ctx],
        )

    def remote(piece, to):
        a, b, s, r = piece
        return pltpu.make_async_remote_copy(
            src_ref=a, dst_ref=b, send_sem=s, recv_sem=r, device_id=(grp, to, ten), device_id_type=MESH
        )

    def skip_copy(k):
        j = lax.rem(ten + k, n_ten)
        return pltpu.make_async_remote_copy(
            src_ref=skip_stage.at[:, pl.ds(pl.multiple_of(j * sub, 128), sub)], dst_ref=skip_rx,
            send_sem=send_skip.at[k], recv_sem=recv_skip.at[0], device_id=(grp, ctx, j), device_id_type=MESH,
        )

    def start_along(h, k):
        to, piece = along(h, k)

        @pl.when(to != ctx)
        def _():
            remote(piece, to).start()

        @pl.when(to == ctx)
        def _():
            pltpu.make_async_copy(piece[0], piece[1], piece[3]).start()

    for k in range(1, n_ten):
        across(0, k).start()
    start_along(0, 0)

    @pl.when(ten == ctx)
    def _():
        for k in range(1, n_ten):
            skip_copy(k).start()
        pltpu.make_async_copy(
            skip_stage.at[:, pl.ds(pl.multiple_of(ten * sub, 128), sub)], skip_rx, recv_skip.at[0]
        ).start()

    for h in range(PARTS):
        if h + 1 < PARTS:
            for k in range(1, n_ten):
                across(h + 1, k).start()
        for k in range(1, n_ten):
            landed(mid.at[h, k], recv_x.at[h, k])
            start_along(h, k)
        if h + 1 < PARTS:
            start_along(h + 1, 0)

    for load in loads[:4]:
        load.wait()
    landed(skip_rx, recv_skip.at[0])

    def gather_copy(h, k):
        here = feats.at[:, pl.ds(pl.multiple_of(ten * sub + h * part, 128), part)]
        return pltpu.make_async_remote_copy(
            src_ref=here, dst_ref=here, send_sem=send2.at[h, k], recv_sem=recv2.at[h, k],
            device_id=(grp, ctx, lax.rem(ten + k, n_ten)), device_id_type=MESH,
        )

    for h in range(PARTS):
        for p in range(n_ctx):
            landed(rx.at[h, :, pl.ds(p * positions, positions), :], recv1.at[h, p])
        acc[...] = jnp.zeros_like(acc)

        @pl.loop(0, length // BLOCK)
        def _(b):
            rows = pl.ds(pl.multiple_of(b * 2 * BLOCK, 2 * BLOCK), 2 * BLOCK)
            f_high, f_low = fh[rows, :], fl[rows, :]
            signal, kernel = rx[h, 0], rx[h, 2]
            spec_s = mm(f_high, signal) + mm(f_low, signal)
            spec_k = mm(f_high, kernel) + mm(f_low, kernel)
            s_re, s_im = spec_s[:BLOCK], spec_s[BLOCK:]
            k_re, k_im = spec_k[:BLOCK], spec_k[BLOCK:]
            prod = jnp.concatenate([s_re * k_re - s_im * k_im, s_re * k_im + s_im * k_re], axis=0)
            p_high = prod.astype(jnp.bfloat16)
            p_low = (prod - p_high.astype(jnp.float32)).astype(jnp.bfloat16)
            g_high, g_low = gh[:, rows], gl[:, rows]
            acc[...] += mm(g_high, p_high) + mm(g_low, p_high) + mm(g_high, p_low)

        skip = skip_rx[0:1, h * part:(h + 1) * part]
        gated = rx[h, 1].astype(jnp.float32) * (
            acc[...] * (1.0 / length) + skip * rx[h, 0].astype(jnp.float32)
        )
        feats[:, pl.ds(pl.multiple_of(ten * sub + h * part, 128), part)] = gated.astype(jnp.bfloat16)
        for k in range(1, n_ten):
            gather_copy(h, k).start()

    loads[4].wait()
    for h in range(PARTS):
        for k in range(1, n_ten):
            came = lax.rem(ten + n_ten - k, n_ten)
            landed(feats.at[:, pl.ds(pl.multiple_of(came * sub + h * part, 128), part)], recv2.at[h, k])

    def partial_copy(k):
        return pltpu.make_async_remote_copy(
            src_ref=pbuf.at[k], dst_ref=rbuf.at[k], send_sem=send3.at[k], recv_sem=recv3.at[k],
            device_id=(grp, lax.rem(ctx + k, n_ctx), ten), device_id_type=MESH,
        )

    order = sorted(range(1, n_ctx), key=lambda k: abs(k - n_ctx / 2))
    for k in order + [0]:
        q = lax.rem(ctx + k, n_ctx)
        rows = pl.ds(pl.multiple_of(q * positions, positions), positions)

        @pl.loop(0, columns // TILE)
        def _(n):
            cols = pl.ds(pl.multiple_of(n * TILE, TILE), TILE)
            product = mm(feats[rows, :], w[:, cols])
            if k == 0:
                own[:, cols] = product
            else:
                pbuf[k, :, cols] = product.astype(jnp.bfloat16)

        if k:
            partial_copy(k).start()

    result = own[...]
    for k in order:
        landed(rbuf.at[k], recv3.at[k])
        result = result + rbuf[k].astype(jnp.float32)
    out_ref[...] = result.astype(jnp.bfloat16)

    @pl.when(ten == ctx)
    def _():
        for k in range(1, n_ten):
            skip_copy(k).wait_send()

    def finish_along(h, k):
        to, piece = along(h, k)

        @pl.when(to != ctx)
        def _():
            remote(piece, to).wait_send()

    for h in range(PARTS):
        for k in range(1, n_ten):
            across(h, k).wait_send()
        for k in range(n_ten):
            finish_along(h, k)
    for h in range(PARTS):
        for k in range(1, n_ten):
            gather_copy(h, k).wait_send()
    for k in order:
        partial_copy(k).wait_send()


def body(outer_gate, inner_gate, value_path, long_filter, skip_scale, out_weight):
    n_ctx = lax.axis_size("context")
    n_ten = lax.axis_size("tensor")
    positions, width = inner_gate.shape
    sub = width // n_ctx
    length = n_ctx * positions
    columns = out_weight.shape[1] // n_ten
    if n_ctx != n_ten or sub % (PARTS * 128) or length % BLOCK or columns % TILE or positions % 16 or length > 1024:
        return body_plain(outer_gate, inner_gate, value_path, long_filter, skip_scale, out_weight)
    tables = [jnp.asarray(t) for t in blocked_tables(length)]
    bf16, f32 = jnp.bfloat16, jnp.float32
    part = sub // PARTS
    dma = pltpu.SemaphoreType.DMA
    vmem = pl.BlockSpec(memory_space=pltpu.VMEM)
    hbm = pl.BlockSpec(memory_space=pl.ANY)
    return pl.pallas_call(
        functools.partial(fused, n_ctx, n_ten),
        out_shape=jax.ShapeDtypeStruct((positions, columns), bf16),
        in_specs=[vmem] * 5 + [hbm] * 5,
        out_specs=vmem,
        scratch_shapes=[
            pltpu.VMEM((out_weight.shape[0], columns), bf16),
            pltpu.VMEM((2 * length, length), bf16),
            pltpu.VMEM((2 * length, length), bf16),
            pltpu.VMEM((length, 2 * length), bf16),
            pltpu.VMEM((length, 2 * length), bf16),
            pltpu.VMEM((3, positions, width), bf16),
            pltpu.VMEM((PARTS, n_ten, 3, positions, part), bf16),
            pltpu.VMEM((PARTS, 3, length, part), bf16),
            pltpu.VMEM((8, width), f32),
            pltpu.VMEM((8, sub), f32),
            pltpu.VMEM((length, part), f32),
            pltpu.VMEM((length, n_ten * sub), bf16),
            pltpu.VMEM((n_ctx, positions, columns), bf16),
            pltpu.VMEM((n_ctx, positions, columns), bf16),
            pltpu.VMEM((positions, columns), f32),
            dma((5,)),
            dma((PARTS, n_ten)), dma((PARTS, n_ten)),
            dma((PARTS, n_ten)), dma((PARTS, n_ctx)),
            dma((n_ten,)), dma((1,)),
            dma((PARTS, n_ten)), dma((PARTS, n_ten)),
            dma((n_ctx,)), dma((n_ctx,)),
        ],
        compiler_params=pltpu.CompilerParams(
            collective_id=0, has_side_effects=True, vmem_limit_bytes=56 * 1024 * 1024
        ),
    )(outer_gate, inner_gate, value_path, long_filter, skip_scale[None, :], out_weight, *tables)


def solution(mesh):
    placed = (
        P(("groups", "context"), "tensor"),
        P(("groups", "context"), "tensor"),
        P(("groups", "context"), "tensor"),
        P("context", "tensor"),
        P("tensor"),
        P("context", None),
    )
    return jax.shard_map(
        body,
        mesh=mesh,
        in_specs=placed,
        out_specs=P(("groups", "context"), "tensor"),
        check_vma=False,
    )
```

```python
import functools
import math

import jax
import jax.numpy as jnp
import ml_dtypes
import numpy as np
from jax import lax
from jax.experimental import pallas as pl
from jax.experimental.pallas import tpu as pltpu
from jax.sharding import PartitionSpec as P


def transform_tables(length):
    index = np.arange(length, dtype=np.int64)
    turns = ((4 * index[:, None] + 1) * index[None, :]) % (4 * length)
    angle = turns * (2.0 * math.pi / (4 * length))
    table = np.concatenate([np.cos(angle), -np.sin(angle)], axis=0)
    high = table.astype(ml_dtypes.bfloat16)
    low = (table - high.astype(np.float64)).astype(ml_dtypes.bfloat16)
    return high, low


def mm(a, b):
    return jnp.dot(a, b, preferred_element_type=jnp.float32)


def causal_conv(high, low, high_t, low_t, signal, kernel):
    length = signal.shape[0]
    spec_s = mm(high, signal) + mm(low, signal)
    spec_k = mm(high, kernel) + mm(low, kernel)
    s_re, s_im = spec_s[:length], spec_s[length:]
    k_re, k_im = spec_k[:length], spec_k[length:]
    prod = jnp.concatenate([s_re * k_re - s_im * k_im, s_re * k_im + s_im * k_re], axis=0)
    p_high = prod.astype(jnp.bfloat16)
    p_low = (prod - p_high.astype(jnp.float32)).astype(jnp.bfloat16)
    return (mm(high_t, p_high) + mm(low_t, p_high) + mm(high_t, p_low)) * (1.0 / length)


def body_plain(outer_gate, inner_gate, value_path, long_filter, skip_scale, out_weight):
    n_ctx = lax.axis_size("context")
    n_ten = lax.axis_size("tensor")
    ctx = lax.axis_index("context")
    ten = lax.axis_index("tensor")
    positions, width = inner_gate.shape
    sub = width // n_ctx
    length = n_ctx * positions
    high, low = transform_tables(length)
    mixed = (inner_gate.astype(jnp.float32) * value_path.astype(jnp.float32)).astype(jnp.bfloat16)
    stacked = jnp.stack([mixed, outer_gate, long_filter])
    stacked = lax.all_to_all(stacked, "context", split_axis=2, concat_axis=1, tiled=True)
    signal, outer, kernel = stacked[0], stacked[1], stacked[2]
    conv = causal_conv(high, low, np.ascontiguousarray(high.T), np.ascontiguousarray(low.T), signal, kernel)
    skip = lax.dynamic_slice_in_dim(skip_scale, ctx * sub, sub, 0)
    gated = (
        outer.astype(jnp.float32) * (conv + skip[None, :] * signal.astype(jnp.float32))
    ).astype(jnp.bfloat16)
    pairs = [(c * n_ten + t, t * n_ctx + c) for c in range(n_ctx) for t in range(n_ten)]
    gated = lax.ppermute(gated, ("context", "tensor"), pairs)
    features = lax.all_gather(gated, "tensor", axis=1, tiled=True)
    columns = out_weight.shape[1] // n_ten
    own = lax.dynamic_slice_in_dim(out_weight, ten * columns, columns, 1)
    partial = mm(features, own).astype(jnp.bfloat16).reshape(n_ctx, positions, columns)
    partial = lax.all_to_all(partial, "context", split_axis=0, concat_axis=0, tiled=True)
    return jnp.sum(partial.astype(jnp.float32), axis=0).astype(jnp.bfloat16)


MESH = pl.DeviceIdType.MESH
PARTS = 2
BLOCK = 128
TILE = 256


def blocked_tables(length):
    high, low = transform_tables(length)

    def order(table):
        halves = table.reshape(2, length // BLOCK, BLOCK, length)
        return np.ascontiguousarray(halves.transpose(1, 0, 2, 3).reshape(2 * length, length))

    high, low = order(high), order(low)
    return high, low, np.ascontiguousarray(high.T), np.ascontiguousarray(low.T)


def fused(
    n_ctx, n_ten,
    outer_ref, inner_ref, value_ref, filter_ref, skip_ref, w_hbm, fh_hbm, fl_hbm, gh_hbm, gl_hbm,
    out_ref,
    w, fh, fl, gh, gl, stage, mid, rx, skip_stage, skip_rx, acc, feats, pbuf, rbuf, own, held,
    load_sem, send_x, recv_x, send1, recv1, send_skip, recv_skip, send2, recv2, send3, recv3,
):
    ctx = lax.axis_index("context")
    ten = lax.axis_index("tensor")
    grp = lax.axis_index("groups")
    positions, width = inner_ref.shape
    sub = width // n_ctx
    part = sub // PARTS
    length = n_ctx * positions
    columns = w.shape[1]

    loads = [
        pltpu.make_async_copy(a, b, load_sem.at[i])
        for i, (a, b) in enumerate(
            [
                (fh_hbm, fh), (fl_hbm, fl), (gh_hbm, gh), (gl_hbm, gl),
                (w_hbm.at[:, pl.ds(pl.multiple_of(ten * columns, 128), columns)], w),
            ]
        )
    ]
    for load in loads:
        load.start()

    barrier = pltpu.get_barrier_semaphore()
    for k in range(1, n_ten):
        pl.semaphore_signal(
            barrier, inc=1, device_id=(grp, ctx, lax.rem(ten + k, n_ten)), device_id_type=MESH
        )
    for k in range(1, n_ctx):
        pl.semaphore_signal(
            barrier, inc=1, device_id=(grp, lax.rem(ctx + k, n_ctx), ten), device_id_type=MESH
        )
    stage[0] = (inner_ref[...].astype(jnp.float32) * value_ref[...].astype(jnp.float32)).astype(jnp.bfloat16)
    stage[1] = outer_ref[...]
    stage[2] = filter_ref[...]
    skip_stage[...] = jnp.broadcast_to(skip_ref[...], skip_stage.shape)
    pl.semaphore_wait(barrier, n_ten + n_ctx - 2)

    def landed(ref, sem):
        pltpu.make_async_copy(ref, ref, sem).wait()

    def slab(j, h):
        return stage.at[:, :, pl.ds(pl.multiple_of(j * sub + h * part, 128), part)]

    def across(h, k):
        j = lax.rem(ten + k, n_ten)
        return pltpu.make_async_remote_copy(
            src_ref=slab(j, h), dst_ref=mid.at[h, k], send_sem=send_x.at[h, k], recv_sem=recv_x.at[h, k],
            device_id=(grp, ctx, j), device_id_type=MESH,
        )

    def along(h, k):
        return lax.rem(ten + n_ten - k, n_ten), (
            mid.at[h, k] if k else slab(ten, h),
            rx.at[h, :, pl.ds(pl.multiple_of(ctx * positions, positions), positions), :],
            send1.at[h, k], recv1.at[h, ctx],
        )

    def remote(piece, to):
        a, b, s, r = piece
        return pltpu.make_async_remote_copy(
            src_ref=a, dst_ref=b, send_sem=s, recv_sem=r, device_id=(grp, to, ten), device_id_type=MESH
        )

    def skip_copy(k):
        j = lax.rem(ten + k, n_ten)
        return pltpu.make_async_remote_copy(
            src_ref=skip_stage.at[:, pl.ds(pl.multiple_of(j * sub, 128), sub)], dst_ref=skip_rx,
            send_sem=send_skip.at[k], recv_sem=recv_skip.at[0], device_id=(grp, ctx, j), device_id_type=MESH,
        )

    def start_along(h, k):
        to, piece = along(h, k)

        @pl.when(to != ctx)
        def _():
            remote(piece, to).start()

        @pl.when(to == ctx)
        def _():
            pltpu.make_async_copy(piece[0], piece[1], piece[3]).start()

    for k in range(1, n_ten):
        across(0, k).start()
    start_along(0, 0)

    @pl.when(ten == ctx)
    def _():
        for k in range(1, n_ten):
            skip_copy(k).start()
        pltpu.make_async_copy(
            skip_stage.at[:, pl.ds(pl.multiple_of(ten * sub, 128), sub)], skip_rx, recv_skip.at[0]
        ).start()

    for h in range(PARTS):
        if h + 1 < PARTS:
            for k in range(1, n_ten):
                across(h + 1, k).start()
        for k in range(1, n_ten):
            landed(mid.at[h, k], recv_x.at[h, k])
            start_along(h, k)
        if h + 1 < PARTS:
            start_along(h + 1, 0)

    for load in loads[:4]:
        load.wait()
    landed(skip_rx, recv_skip.at[0])

    def gather_copy(h, k):
        here = feats.at[:, pl.ds(pl.multiple_of(ten * sub + h * part, 128), part)]
        return pltpu.make_async_remote_copy(
            src_ref=here, dst_ref=here, send_sem=send2.at[h, k], recv_sem=recv2.at[h, k],
            device_id=(grp, ctx, lax.rem(ten + k, n_ten)), device_id_type=MESH,
        )

    for h in range(PARTS):
        for p in range(n_ctx):
            landed(rx.at[h, :, pl.ds(p * positions, positions), :], recv1.at[h, p])
        acc[...] = jnp.zeros_like(acc)

        @pl.loop(0, length // BLOCK)
        def _(b):
            rows = pl.ds(pl.multiple_of(b * 2 * BLOCK, 2 * BLOCK), 2 * BLOCK)
            f_high, f_low = fh[rows, :], fl[rows, :]
            signal, kernel = rx[h, 0], rx[h, 2]
            spec_s = mm(f_high, signal) + mm(f_low, signal)
            spec_k = mm(f_high, kernel) + mm(f_low, kernel)
            s_re, s_im = spec_s[:BLOCK], spec_s[BLOCK:]
            k_re, k_im = spec_k[:BLOCK], spec_k[BLOCK:]
            prod = jnp.concatenate([s_re * k_re - s_im * k_im, s_re * k_im + s_im * k_re], axis=0)
            p_high = prod.astype(jnp.bfloat16)
            p_low = (prod - p_high.astype(jnp.float32)).astype(jnp.bfloat16)
            g_high, g_low = gh[:, rows], gl[:, rows]
            acc[...] += mm(g_high, p_high) + mm(g_low, p_high) + mm(g_high, p_low)

        skip = skip_rx[0:1, h * part:(h + 1) * part]
        gated = rx[h, 1].astype(jnp.float32) * (
            acc[...] * (1.0 / length) + skip * rx[h, 0].astype(jnp.float32)
        )
        feats[:, pl.ds(pl.multiple_of(ten * sub + h * part, 128), part)] = gated.astype(jnp.bfloat16)
        for k in range(1, n_ten):
            gather_copy(h, k).start()

    loads[4].wait()
    for h in range(PARTS):
        for k in range(1, n_ten):
            came = lax.rem(ten + n_ten - k, n_ten)
            landed(feats.at[:, pl.ds(pl.multiple_of(came * sub + h * part, 128), part)], recv2.at[h, k])

    def partial_copy(q, to, slot):
        return pltpu.make_async_remote_copy(
            src_ref=pbuf.at[q], dst_ref=rbuf.at[slot], send_sem=send3.at[q], recv_sem=recv3.at[slot],
            device_id=(grp, to, ten), device_id_type=MESH,
        )

    def project(q, dest):
        @pl.loop(0, columns // TILE)
        def _(n):
            cols = pl.ds(pl.multiple_of(n * TILE, TILE), TILE)
            product = mm(feats[q * positions:(q + 1) * positions, :], w[:, cols])
            dest[:, cols] = product.astype(dest.dtype)

    def exchange(role):
        copies = []

        def send(q, to, slot):
            copies.append(partial_copy(q, to, slot))
            copies[-1].start()

        if role in (0, 3):
            near, third, far = (1, 2, 3) if role == 0 else (2, 1, 0)
            project(far, pbuf.at[far])
            send(far, near, near)
            project(third, pbuf.at[third])
            send(third, third, role)
            project(near, pbuf.at[near])
            send(near, near, role)
            project(role, own)
            expected = (near, third)
        else:
            peer = 3 - role
            near = 0 if role == 1 else 3
            far = 3 - near
            project(peer, pbuf.at[peer])
            send(peer, peer, role)
            project(far, held)
            project(near, pbuf.at[near])
            send(near, near, role)
            project(role, own)
            landed(rbuf.at[role], recv3.at[role])
            pbuf[far] = (held[...] + rbuf[role].astype(jnp.float32)).astype(jnp.bfloat16)
            send(far, far, role)
            expected = (near, peer, far)
        result = own[...]
        for slot in expected:
            landed(rbuf.at[slot], recv3.at[slot])
            result = result + rbuf[slot].astype(jnp.float32)
        out_ref[...] = result.astype(jnp.bfloat16)
        for copy in copies:
            copy.wait_send()

    for role in range(n_ctx):

        @pl.when(ctx == role)
        def _():
            exchange(role)

    @pl.when(ten == ctx)
    def _():
        for k in range(1, n_ten):
            skip_copy(k).wait_send()

    def finish_along(h, k):
        to, piece = along(h, k)

        @pl.when(to != ctx)
        def _():
            remote(piece, to).wait_send()

    for h in range(PARTS):
        for k in range(1, n_ten):
            across(h, k).wait_send()
        for k in range(n_ten):
            finish_along(h, k)
    for h in range(PARTS):
        for k in range(1, n_ten):
            gather_copy(h, k).wait_send()


def body(outer_gate, inner_gate, value_path, long_filter, skip_scale, out_weight):
    n_ctx = lax.axis_size("context")
    n_ten = lax.axis_size("tensor")
    positions, width = inner_gate.shape
    sub = width // n_ctx
    length = n_ctx * positions
    columns = out_weight.shape[1] // n_ten
    if n_ctx != 4 or n_ctx != n_ten or sub % (PARTS * 128) or length % BLOCK or columns % TILE or positions % 16 or length > 1024:
        return body_plain(outer_gate, inner_gate, value_path, long_filter, skip_scale, out_weight)
    tables = [jnp.asarray(t) for t in blocked_tables(length)]
    bf16, f32 = jnp.bfloat16, jnp.float32
    part = sub // PARTS
    dma = pltpu.SemaphoreType.DMA
    vmem = pl.BlockSpec(memory_space=pltpu.VMEM)
    hbm = pl.BlockSpec(memory_space=pl.ANY)
    return pl.pallas_call(
        functools.partial(fused, n_ctx, n_ten),
        out_shape=jax.ShapeDtypeStruct((positions, columns), bf16),
        in_specs=[vmem] * 5 + [hbm] * 5,
        out_specs=vmem,
        scratch_shapes=[
            pltpu.VMEM((out_weight.shape[0], columns), bf16),
            pltpu.VMEM((2 * length, length), bf16),
            pltpu.VMEM((2 * length, length), bf16),
            pltpu.VMEM((length, 2 * length), bf16),
            pltpu.VMEM((length, 2 * length), bf16),
            pltpu.VMEM((3, positions, width), bf16),
            pltpu.VMEM((PARTS, n_ten, 3, positions, part), bf16),
            pltpu.VMEM((PARTS, 3, length, part), bf16),
            pltpu.VMEM((8, width), f32),
            pltpu.VMEM((8, sub), f32),
            pltpu.VMEM((length, part), f32),
            pltpu.VMEM((length, n_ten * sub), bf16),
            pltpu.VMEM((n_ctx, positions, columns), bf16),
            pltpu.VMEM((n_ctx, positions, columns), bf16),
            pltpu.VMEM((positions, columns), f32),
            pltpu.VMEM((positions, columns), f32),
            dma((5,)),
            dma((PARTS, n_ten)), dma((PARTS, n_ten)),
            dma((PARTS, n_ten)), dma((PARTS, n_ctx)),
            dma((n_ten,)), dma((1,)),
            dma((PARTS, n_ten)), dma((PARTS, n_ten)),
            dma((n_ctx,)), dma((n_ctx,)),
        ],
        compiler_params=pltpu.CompilerParams(
            collective_id=0, has_side_effects=True, vmem_limit_bytes=56 * 1024 * 1024
        ),
    )(outer_gate, inner_gate, value_path, long_filter, skip_scale[None, :], out_weight, *tables)


def solution(mesh):
    placed = (
        P(("groups", "context"), "tensor"),
        P(("groups", "context"), "tensor"),
        P(("groups", "context"), "tensor"),
        P("context", "tensor"),
        P("tensor"),
        P("context", None),
    )
    return jax.shard_map(
        body,
        mesh=mesh,
        in_specs=placed,
        out_specs=P(("groups", "context"), "tensor"),
        check_vma=False,
    )
```

```python
import functools
import math

import jax
import jax.numpy as jnp
import ml_dtypes
import numpy as np
from jax import lax
from jax.experimental import pallas as pl
from jax.experimental.pallas import tpu as pltpu
from jax.sharding import PartitionSpec as P


def transform_tables(length):
    index = np.arange(length, dtype=np.int64)
    turns = ((4 * index[:, None] + 1) * index[None, :]) % (4 * length)
    angle = turns * (2.0 * math.pi / (4 * length))
    table = np.concatenate([np.cos(angle), -np.sin(angle)], axis=0)
    high = table.astype(ml_dtypes.bfloat16)
    low = (table - high.astype(np.float64)).astype(ml_dtypes.bfloat16)
    return high, low


def mm(a, b):
    return jnp.dot(a, b, preferred_element_type=jnp.float32)


def causal_conv(high, low, high_t, low_t, signal, kernel):
    length = signal.shape[0]
    spec_s = mm(high, signal) + mm(low, signal)
    spec_k = mm(high, kernel) + mm(low, kernel)
    s_re, s_im = spec_s[:length], spec_s[length:]
    k_re, k_im = spec_k[:length], spec_k[length:]
    prod = jnp.concatenate([s_re * k_re - s_im * k_im, s_re * k_im + s_im * k_re], axis=0)
    p_high = prod.astype(jnp.bfloat16)
    p_low = (prod - p_high.astype(jnp.float32)).astype(jnp.bfloat16)
    return (mm(high_t, p_high) + mm(low_t, p_high) + mm(high_t, p_low)) * (1.0 / length)


def body_plain(outer_gate, inner_gate, value_path, long_filter, skip_scale, out_weight):
    n_ctx = lax.axis_size("context")
    n_ten = lax.axis_size("tensor")
    ctx = lax.axis_index("context")
    ten = lax.axis_index("tensor")
    positions, width = inner_gate.shape
    sub = width // n_ctx
    length = n_ctx * positions
    high, low = transform_tables(length)
    mixed = (inner_gate.astype(jnp.float32) * value_path.astype(jnp.float32)).astype(jnp.bfloat16)
    stacked = jnp.stack([mixed, outer_gate, long_filter])
    stacked = lax.all_to_all(stacked, "context", split_axis=2, concat_axis=1, tiled=True)
    signal, outer, kernel = stacked[0], stacked[1], stacked[2]
    conv = causal_conv(high, low, np.ascontiguousarray(high.T), np.ascontiguousarray(low.T), signal, kernel)
    skip = lax.dynamic_slice_in_dim(skip_scale, ctx * sub, sub, 0)
    gated = (
        outer.astype(jnp.float32) * (conv + skip[None, :] * signal.astype(jnp.float32))
    ).astype(jnp.bfloat16)
    pairs = [(c * n_ten + t, t * n_ctx + c) for c in range(n_ctx) for t in range(n_ten)]
    gated = lax.ppermute(gated, ("context", "tensor"), pairs)
    features = lax.all_gather(gated, "tensor", axis=1, tiled=True)
    columns = out_weight.shape[1] // n_ten
    own = lax.dynamic_slice_in_dim(out_weight, ten * columns, columns, 1)
    partial = mm(features, own).astype(jnp.bfloat16).reshape(n_ctx, positions, columns)
    partial = lax.all_to_all(partial, "context", split_axis=0, concat_axis=0, tiled=True)
    return jnp.sum(partial.astype(jnp.float32), axis=0).astype(jnp.bfloat16)


MESH = pl.DeviceIdType.MESH
PARTS = 4
BLOCK = 128
TILE = 256


def blocked_tables(length):
    high, low = transform_tables(length)

    def order(table):
        halves = table.reshape(2, length // BLOCK, BLOCK, length)
        return np.ascontiguousarray(halves.transpose(1, 0, 2, 3).reshape(2 * length, length))

    high, low = order(high), order(low)
    return high, low, np.ascontiguousarray(high.T), np.ascontiguousarray(low.T)


def fused(
    n_ctx, n_ten,
    outer_ref, inner_ref, value_ref, filter_ref, skip_ref, w_hbm, fh_hbm, fl_hbm, gh_hbm, gl_hbm,
    out_ref,
    w, fh, fl, gh, gl, stage, mid, rx, skip_stage, skip_rx, acc, feats, pbuf, rbuf, own, held,
    load_sem, send_x, recv_x, send1, recv1, send_skip, recv_skip, send2, recv2, send3, recv3,
):
    ctx = lax.axis_index("context")
    ten = lax.axis_index("tensor")
    grp = lax.axis_index("groups")
    positions, width = inner_ref.shape
    sub = width // n_ctx
    part = sub // PARTS
    length = n_ctx * positions
    columns = w.shape[1]

    loads = [
        pltpu.make_async_copy(a, b, load_sem.at[i])
        for i, (a, b) in enumerate(
            [
                (fh_hbm, fh), (fl_hbm, fl), (gh_hbm, gh), (gl_hbm, gl),
                (w_hbm.at[:, pl.ds(pl.multiple_of(ten * columns, 128), columns)], w),
            ]
        )
    ]
    for load in loads:
        load.start()

    barrier = pltpu.get_barrier_semaphore()
    for k in range(1, n_ten):
        pl.semaphore_signal(
            barrier, inc=1, device_id=(grp, ctx, lax.rem(ten + k, n_ten)), device_id_type=MESH
        )
    for k in range(1, n_ctx):
        pl.semaphore_signal(
            barrier, inc=1, device_id=(grp, lax.rem(ctx + k, n_ctx), ten), device_id_type=MESH
        )
    stage[0] = (inner_ref[...].astype(jnp.float32) * value_ref[...].astype(jnp.float32)).astype(jnp.bfloat16)
    stage[1] = outer_ref[...]
    stage[2] = filter_ref[...]
    skip_stage[...] = jnp.broadcast_to(skip_ref[...], skip_stage.shape)
    pl.semaphore_wait(barrier, n_ten + n_ctx - 2)

    def landed(ref, sem):
        pltpu.make_async_copy(ref, ref, sem).wait()

    def slab(j, h):
        return stage.at[:, :, pl.ds(pl.multiple_of(j * sub + h * part, 128), part)]

    def across(h, k):
        j = lax.rem(ten + k, n_ten)
        return pltpu.make_async_remote_copy(
            src_ref=slab(j, h), dst_ref=mid.at[h, k], send_sem=send_x.at[h, k], recv_sem=recv_x.at[h, k],
            device_id=(grp, ctx, j), device_id_type=MESH,
        )

    def along(h, k):
        return lax.rem(ten + n_ten - k, n_ten), (
            mid.at[h, k] if k else slab(ten, h),
            rx.at[h, :, pl.ds(pl.multiple_of(ctx * positions, positions), positions), :],
            send1.at[h, k], recv1.at[h, ctx],
        )

    def remote(piece, to):
        a, b, s, r = piece
        return pltpu.make_async_remote_copy(
            src_ref=a, dst_ref=b, send_sem=s, recv_sem=r, device_id=(grp, to, ten), device_id_type=MESH
        )

    def skip_copy(k):
        j = lax.rem(ten + k, n_ten)
        return pltpu.make_async_remote_copy(
            src_ref=skip_stage.at[:, pl.ds(pl.multiple_of(j * sub, 128), sub)], dst_ref=skip_rx,
            send_sem=send_skip.at[k], recv_sem=recv_skip.at[0], device_id=(grp, ctx, j), device_id_type=MESH,
        )

    def start_along(h, k):
        to, piece = along(h, k)

        @pl.when(to != ctx)
        def _():
            remote(piece, to).start()

        @pl.when(to == ctx)
        def _():
            pltpu.make_async_copy(piece[0], piece[1], piece[3]).start()

    for k in range(1, n_ten):
        across(0, k).start()
    start_along(0, 0)

    @pl.when(ten == ctx)
    def _():
        for k in range(1, n_ten):
            skip_copy(k).start()
        pltpu.make_async_copy(
            skip_stage.at[:, pl.ds(pl.multiple_of(ten * sub, 128), sub)], skip_rx, recv_skip.at[0]
        ).start()

    for h in range(PARTS):
        if h + 1 < PARTS:
            for k in range(1, n_ten):
                across(h + 1, k).start()
        for k in range(1, n_ten):
            landed(mid.at[h, k], recv_x.at[h, k])
            start_along(h, k)
        if h + 1 < PARTS:
            start_along(h + 1, 0)

    for load in loads[:4]:
        load.wait()
    landed(skip_rx, recv_skip.at[0])

    def gather_copy(h, k):
        here = feats.at[:, pl.ds(pl.multiple_of(ten * sub + h * part, 128), part)]
        return pltpu.make_async_remote_copy(
            src_ref=here, dst_ref=here, send_sem=send2.at[h, k], recv_sem=recv2.at[h, k],
            device_id=(grp, ctx, lax.rem(ten + k, n_ten)), device_id_type=MESH,
        )

    for h in range(PARTS):
        for p in range(n_ctx):
            landed(rx.at[h, :, pl.ds(p * positions, positions), :], recv1.at[h, p])
        acc[...] = jnp.zeros_like(acc)

        @pl.loop(0, length // BLOCK)
        def _(b):
            rows = pl.ds(pl.multiple_of(b * 2 * BLOCK, 2 * BLOCK), 2 * BLOCK)
            f_high, f_low = fh[rows, :], fl[rows, :]
            signal, kernel = rx[h, 0], rx[h, 2]
            spec_s = mm(f_high, signal) + mm(f_low, signal)
            spec_k = mm(f_high, kernel) + mm(f_low, kernel)
            s_re, s_im = spec_s[:BLOCK], spec_s[BLOCK:]
            k_re, k_im = spec_k[:BLOCK], spec_k[BLOCK:]
            prod = jnp.concatenate([s_re * k_re - s_im * k_im, s_re * k_im + s_im * k_re], axis=0)
            p_high = prod.astype(jnp.bfloat16)
            p_low = (prod - p_high.astype(jnp.float32)).astype(jnp.bfloat16)
            g_high, g_low = gh[:, rows], gl[:, rows]
            acc[...] += mm(g_high, p_high) + mm(g_low, p_high) + mm(g_high, p_low)

        skip = skip_rx[0:1, h * part:(h + 1) * part]
        gated = rx[h, 1].astype(jnp.float32) * (
            acc[...] * (1.0 / length) + skip * rx[h, 0].astype(jnp.float32)
        )
        feats[:, pl.ds(pl.multiple_of(ten * sub + h * part, 128), part)] = gated.astype(jnp.bfloat16)
        for k in range(1, n_ten):
            gather_copy(h, k).start()

    loads[4].wait()
    for h in range(PARTS):
        for k in range(1, n_ten):
            came = lax.rem(ten + n_ten - k, n_ten)
            landed(feats.at[:, pl.ds(pl.multiple_of(came * sub + h * part, 128), part)], recv2.at[h, k])

    def partial_copy(q, to, slot):
        return pltpu.make_async_remote_copy(
            src_ref=pbuf.at[q], dst_ref=rbuf.at[slot], send_sem=send3.at[q], recv_sem=recv3.at[slot],
            device_id=(grp, to, ten), device_id_type=MESH,
        )

    def project(q, dest):
        @pl.loop(0, columns // TILE)
        def _(n):
            cols = pl.ds(pl.multiple_of(n * TILE, TILE), TILE)
            product = mm(feats[q * positions:(q + 1) * positions, :], w[:, cols])
            dest[:, cols] = product.astype(dest.dtype)

    def exchange(role):
        copies = []

        def send(q, to, slot):
            copies.append(partial_copy(q, to, slot))
            copies[-1].start()

        if role in (0, 3):
            near, third, far = (1, 2, 3) if role == 0 else (2, 1, 0)
            project(far, pbuf.at[far])
            send(far, near, near)
            project(third, pbuf.at[third])
            send(third, third, role)
            project(near, pbuf.at[near])
            send(near, near, role)
            project(role, own)
            expected = (near, third)
        else:
            peer = 3 - role
            near = 0 if role == 1 else 3
            far = 3 - near
            project(peer, pbuf.at[peer])
            send(peer, peer, role)
            project(far, held)
            project(near, pbuf.at[near])
            send(near, near, role)
            project(role, own)
            landed(rbuf.at[role], recv3.at[role])
            pbuf[far] = (held[...] + rbuf[role].astype(jnp.float32)).astype(jnp.bfloat16)
            send(far, far, role)
            expected = (near, peer, far)
        result = own[...]
        for slot in expected:
            landed(rbuf.at[slot], recv3.at[slot])
            result = result + rbuf[slot].astype(jnp.float32)
        out_ref[...] = result.astype(jnp.bfloat16)
        for copy in copies:
            copy.wait_send()

    for role in range(n_ctx):

        @pl.when(ctx == role)
        def _():
            exchange(role)

    @pl.when(ten == ctx)
    def _():
        for k in range(1, n_ten):
            skip_copy(k).wait_send()

    def finish_along(h, k):
        to, piece = along(h, k)

        @pl.when(to != ctx)
        def _():
            remote(piece, to).wait_send()

    for h in range(PARTS):
        for k in range(1, n_ten):
            across(h, k).wait_send()
        for k in range(n_ten):
            finish_along(h, k)
    for h in range(PARTS):
        for k in range(1, n_ten):
            gather_copy(h, k).wait_send()


def body(outer_gate, inner_gate, value_path, long_filter, skip_scale, out_weight):
    n_ctx = lax.axis_size("context")
    n_ten = lax.axis_size("tensor")
    positions, width = inner_gate.shape
    sub = width // n_ctx
    length = n_ctx * positions
    columns = out_weight.shape[1] // n_ten
    if n_ctx != 4 or n_ctx != n_ten or sub % (PARTS * 128) or length % BLOCK or columns % TILE or positions % 16 or length > 1024:
        return body_plain(outer_gate, inner_gate, value_path, long_filter, skip_scale, out_weight)
    tables = [jnp.asarray(t) for t in blocked_tables(length)]
    bf16, f32 = jnp.bfloat16, jnp.float32
    part = sub // PARTS
    dma = pltpu.SemaphoreType.DMA
    vmem = pl.BlockSpec(memory_space=pltpu.VMEM)
    hbm = pl.BlockSpec(memory_space=pl.ANY)
    return pl.pallas_call(
        functools.partial(fused, n_ctx, n_ten),
        out_shape=jax.ShapeDtypeStruct((positions, columns), bf16),
        in_specs=[vmem] * 5 + [hbm] * 5,
        out_specs=vmem,
        scratch_shapes=[
            pltpu.VMEM((out_weight.shape[0], columns), bf16),
            pltpu.VMEM((2 * length, length), bf16),
            pltpu.VMEM((2 * length, length), bf16),
            pltpu.VMEM((length, 2 * length), bf16),
            pltpu.VMEM((length, 2 * length), bf16),
            pltpu.VMEM((3, positions, width), bf16),
            pltpu.VMEM((PARTS, n_ten, 3, positions, part), bf16),
            pltpu.VMEM((PARTS, 3, length, part), bf16),
            pltpu.VMEM((8, width), f32),
            pltpu.VMEM((8, sub), f32),
            pltpu.VMEM((length, part), f32),
            pltpu.VMEM((length, n_ten * sub), bf16),
            pltpu.VMEM((n_ctx, positions, columns), bf16),
            pltpu.VMEM((n_ctx, positions, columns), bf16),
            pltpu.VMEM((positions, columns), f32),
            pltpu.VMEM((positions, columns), f32),
            dma((5,)),
            dma((PARTS, n_ten)), dma((PARTS, n_ten)),
            dma((PARTS, n_ten)), dma((PARTS, n_ctx)),
            dma((n_ten,)), dma((1,)),
            dma((PARTS, n_ten)), dma((PARTS, n_ten)),
            dma((n_ctx,)), dma((n_ctx,)),
        ],
        compiler_params=pltpu.CompilerParams(
            collective_id=0, has_side_effects=True, vmem_limit_bytes=56 * 1024 * 1024
        ),
    )(outer_gate, inner_gate, value_path, long_filter, skip_scale[None, :], out_weight, *tables)


def solution(mesh):
    placed = (
        P(("groups", "context"), "tensor"),
        P(("groups", "context"), "tensor"),
        P(("groups", "context"), "tensor"),
        P("context", "tensor"),
        P("tensor"),
        P("context", None),
    )
    return jax.shard_map(
        body,
        mesh=mesh,
        in_specs=placed,
        out_specs=P(("groups", "context"), "tensor"),
        check_vma=False,
    )
```

```python
import functools
import math

import jax
import jax.numpy as jnp
import ml_dtypes
import numpy as np
from jax import lax
from jax.experimental import pallas as pl
from jax.experimental.pallas import tpu as pltpu
from jax.sharding import PartitionSpec as P


def transform_tables(length):
    index = np.arange(length, dtype=np.int64)
    turns = ((4 * index[:, None] + 1) * index[None, :]) % (4 * length)
    angle = turns * (2.0 * math.pi / (4 * length))
    table = np.concatenate([np.cos(angle), -np.sin(angle)], axis=0)
    high = table.astype(ml_dtypes.bfloat16)
    low = (table - high.astype(np.float64)).astype(ml_dtypes.bfloat16)
    return high, low


def mm(a, b):
    return jnp.dot(a, b, preferred_element_type=jnp.float32)


def causal_conv(high, low, high_t, low_t, signal, kernel):
    length = signal.shape[0]
    spec_s = mm(high, signal) + mm(low, signal)
    spec_k = mm(high, kernel) + mm(low, kernel)
    s_re, s_im = spec_s[:length], spec_s[length:]
    k_re, k_im = spec_k[:length], spec_k[length:]
    prod = jnp.concatenate([s_re * k_re - s_im * k_im, s_re * k_im + s_im * k_re], axis=0)
    p_high = prod.astype(jnp.bfloat16)
    p_low = (prod - p_high.astype(jnp.float32)).astype(jnp.bfloat16)
    return (mm(high_t, p_high) + mm(low_t, p_high) + mm(high_t, p_low)) * (1.0 / length)


def body_plain(outer_gate, inner_gate, value_path, long_filter, skip_scale, out_weight):
    n_ctx = lax.axis_size("context")
    n_ten = lax.axis_size("tensor")
    ctx = lax.axis_index("context")
    ten = lax.axis_index("tensor")
    positions, width = inner_gate.shape
    sub = width // n_ctx
    length = n_ctx * positions
    high, low = transform_tables(length)
    mixed = (inner_gate.astype(jnp.float32) * value_path.astype(jnp.float32)).astype(jnp.bfloat16)
    stacked = jnp.stack([mixed, outer_gate, long_filter])
    stacked = lax.all_to_all(stacked, "context", split_axis=2, concat_axis=1, tiled=True)
    signal, outer, kernel = stacked[0], stacked[1], stacked[2]
    conv = causal_conv(high, low, np.ascontiguousarray(high.T), np.ascontiguousarray(low.T), signal, kernel)
    skip = lax.dynamic_slice_in_dim(skip_scale, ctx * sub, sub, 0)
    gated = (
        outer.astype(jnp.float32) * (conv + skip[None, :] * signal.astype(jnp.float32))
    ).astype(jnp.bfloat16)
    pairs = [(c * n_ten + t, t * n_ctx + c) for c in range(n_ctx) for t in range(n_ten)]
    gated = lax.ppermute(gated, ("context", "tensor"), pairs)
    features = lax.all_gather(gated, "tensor", axis=1, tiled=True)
    columns = out_weight.shape[1] // n_ten
    own = lax.dynamic_slice_in_dim(out_weight, ten * columns, columns, 1)
    partial = mm(features, own).astype(jnp.bfloat16).reshape(n_ctx, positions, columns)
    partial = lax.all_to_all(partial, "context", split_axis=0, concat_axis=0, tiled=True)
    return jnp.sum(partial.astype(jnp.float32), axis=0).astype(jnp.bfloat16)


MESH = pl.DeviceIdType.MESH
PARTS = 4
BLOCK = 128
TILE = 256


def blocked_tables(length):
    high, low = transform_tables(length)

    def order(table):
        halves = table.reshape(2, length // BLOCK, BLOCK, length)
        return np.ascontiguousarray(halves.transpose(1, 0, 2, 3).reshape(2 * length, length))

    high, low = order(high), order(low)
    return high, low, np.ascontiguousarray(high.T), np.ascontiguousarray(low.T)


def fused(
    n_ctx, n_ten,
    outer_ref, inner_ref, value_ref, filter_ref, skip_ref, w_hbm, fh_hbm, fl_hbm, gh_hbm, gl_hbm,
    out_ref,
    w, fh, fl, gh, gl, stage, mid, rx, skip_stage, skip_rx, acc, feats, pbuf, rbuf, own, held,
    load_sem, send_x, recv_x, send1, recv1, send_skip, recv_skip, send2, recv2, send3, recv3,
):
    ctx = lax.axis_index("context")
    ten = lax.axis_index("tensor")
    grp = lax.axis_index("groups")
    positions, width = inner_ref.shape
    sub = width // n_ctx
    part = sub // PARTS
    length = n_ctx * positions
    columns = w.shape[1]

    loads = [
        pltpu.make_async_copy(a, b, load_sem.at[i])
        for i, (a, b) in enumerate(
            [
                (fh_hbm, fh), (fl_hbm, fl), (gh_hbm, gh), (gl_hbm, gl),
                (w_hbm.at[:, pl.ds(pl.multiple_of(ten * columns, 128), columns)], w),
            ]
        )
    ]
    for load in loads:
        load.start()

    barrier = pltpu.get_barrier_semaphore()
    for k in range(1, n_ten):
        pl.semaphore_signal(
            barrier, inc=1, device_id=(grp, ctx, lax.rem(ten + k, n_ten)), device_id_type=MESH
        )
    for k in range(1, n_ctx):
        pl.semaphore_signal(
            barrier, inc=1, device_id=(grp, lax.rem(ctx + k, n_ctx), ten), device_id_type=MESH
        )
    stage[0] = (inner_ref[...].astype(jnp.float32) * value_ref[...].astype(jnp.float32)).astype(jnp.bfloat16)
    stage[1] = outer_ref[...]
    stage[2] = filter_ref[...]
    skip_stage[...] = jnp.broadcast_to(skip_ref[...], skip_stage.shape)
    pl.semaphore_wait(barrier, n_ten + n_ctx - 2)

    def landed(ref, sem):
        pltpu.make_async_copy(ref, ref, sem).wait()

    def slab(j, h):
        return stage.at[:, :, pl.ds(pl.multiple_of(j * sub + h * part, 128), part)]

    def across(h, k):
        j = lax.rem(ten + k, n_ten)
        return pltpu.make_async_remote_copy(
            src_ref=slab(j, h), dst_ref=mid.at[h, k], send_sem=send_x.at[h, k], recv_sem=recv_x.at[h, k],
            device_id=(grp, ctx, j), device_id_type=MESH,
        )

    def along(h, k):
        return lax.rem(ten + n_ten - k, n_ten), (
            mid.at[h, k] if k else slab(ten, h),
            rx.at[h, :, pl.ds(pl.multiple_of(ctx * positions, positions), positions), :],
            send1.at[h, k], recv1.at[h, ctx],
        )

    def remote(piece, to):
        a, b, s, r = piece
        return pltpu.make_async_remote_copy(
            src_ref=a, dst_ref=b, send_sem=s, recv_sem=r, device_id=(grp, to, ten), device_id_type=MESH
        )

    def skip_copy(k):
        j = lax.rem(ten + k, n_ten)
        return pltpu.make_async_remote_copy(
            src_ref=skip_stage.at[:, pl.ds(pl.multiple_of(j * sub, 128), sub)], dst_ref=skip_rx,
            send_sem=send_skip.at[k], recv_sem=recv_skip.at[0], device_id=(grp, ctx, j), device_id_type=MESH,
        )

    def start_along(h, k):
        to, piece = along(h, k)

        @pl.when(to != ctx)
        def _():
            remote(piece, to).start()

        @pl.when(to == ctx)
        def _():
            pltpu.make_async_copy(piece[0], piece[1], piece[3]).start()

    for k in range(1, n_ten):
        across(0, k).start()
    start_along(0, 0)

    @pl.when(ten == ctx)
    def _():
        for k in range(1, n_ten):
            skip_copy(k).start()
        pltpu.make_async_copy(
            skip_stage.at[:, pl.ds(pl.multiple_of(ten * sub, 128), sub)], skip_rx, recv_skip.at[0]
        ).start()

    for h in range(PARTS):
        if h + 1 < PARTS:
            for k in range(1, n_ten):
                across(h + 1, k).start()
        for k in range(1, n_ten):
            landed(mid.at[h, k], recv_x.at[h, k])
            start_along(h, k)
        if h + 1 < PARTS:
            start_along(h + 1, 0)

    for load in loads[:4]:
        load.wait()
    landed(skip_rx, recv_skip.at[0])

    def gather_copy(h, k):
        here = feats.at[:, pl.ds(pl.multiple_of(ten * sub + h * part, 128), part)]
        return pltpu.make_async_remote_copy(
            src_ref=here, dst_ref=here, send_sem=send2.at[h, k], recv_sem=recv2.at[h, k],
            device_id=(grp, ctx, lax.rem(ten + k, n_ten)), device_id_type=MESH,
        )

    for h in range(PARTS):
        for p in range(n_ctx):
            landed(rx.at[h, :, pl.ds(p * positions, positions), :], recv1.at[h, p])
        acc[...] = jnp.zeros_like(acc)

        @pl.loop(0, length // BLOCK)
        def _(b):
            rows = pl.ds(pl.multiple_of(b * 2 * BLOCK, 2 * BLOCK), 2 * BLOCK)
            f_high, f_low = fh[rows, :], fl[rows, :]
            both = jnp.concatenate([rx[h, 0], rx[h, 2]], axis=1)
            spec = mm(f_high, both) + mm(f_low, both)
            spec_s, spec_k = spec[:, :part], spec[:, part:]
            s_re, s_im = spec_s[:BLOCK], spec_s[BLOCK:]
            k_re, k_im = spec_k[:BLOCK], spec_k[BLOCK:]
            prod = jnp.concatenate([s_re * k_re - s_im * k_im, s_re * k_im + s_im * k_re], axis=0)
            p_high = prod.astype(jnp.bfloat16)
            p_low = (prod - p_high.astype(jnp.float32)).astype(jnp.bfloat16)
            g_high, g_low = gh[:, rows], gl[:, rows]
            acc[...] += mm(g_high, p_high) + mm(g_low, p_high) + mm(g_high, p_low)

        skip = skip_rx[0:1, h * part:(h + 1) * part]
        gated = rx[h, 1].astype(jnp.float32) * (
            acc[...] * (1.0 / length) + skip * rx[h, 0].astype(jnp.float32)
        )
        feats[:, pl.ds(pl.multiple_of(ten * sub + h * part, 128), part)] = gated.astype(jnp.bfloat16)
        for k in range(1, n_ten):
            gather_copy(h, k).start()

    loads[4].wait()
    for h in range(PARTS):
        for k in range(1, n_ten):
            came = lax.rem(ten + n_ten - k, n_ten)
            landed(feats.at[:, pl.ds(pl.multiple_of(came * sub + h * part, 128), part)], recv2.at[h, k])

    def partial_copy(q, to, slot):
        return pltpu.make_async_remote_copy(
            src_ref=pbuf.at[q], dst_ref=rbuf.at[slot], send_sem=send3.at[q], recv_sem=recv3.at[slot],
            device_id=(grp, to, ten), device_id_type=MESH,
        )

    def project(q, dest):
        @pl.loop(0, columns // TILE)
        def _(n):
            cols = pl.ds(pl.multiple_of(n * TILE, TILE), TILE)
            product = mm(feats[q * positions:(q + 1) * positions, :], w[:, cols])
            dest[:, cols] = product.astype(dest.dtype)

    def exchange(role):
        copies = []

        def send(q, to, slot):
            copies.append(partial_copy(q, to, slot))
            copies[-1].start()

        if role in (0, 3):
            near, third, far = (1, 2, 3) if role == 0 else (2, 1, 0)
            project(far, pbuf.at[far])
            send(far, near, near)
            project(third, pbuf.at[third])
            send(third, third, role)
            project(near, pbuf.at[near])
            send(near, near, role)
            project(role, own)
            expected = (near, third)
        else:
            peer = 3 - role
            near = 0 if role == 1 else 3
            far = 3 - near
            project(peer, pbuf.at[peer])
            send(peer, peer, role)
            project(far, held)
            project(near, pbuf.at[near])
            send(near, near, role)
            project(role, own)
            landed(rbuf.at[role], recv3.at[role])
            pbuf[far] = (held[...] + rbuf[role].astype(jnp.float32)).astype(jnp.bfloat16)
            send(far, far, role)
            expected = (near, peer, far)
        result = own[...]
        for slot in expected:
            landed(rbuf.at[slot], recv3.at[slot])
            result = result + rbuf[slot].astype(jnp.float32)
        out_ref[...] = result.astype(jnp.bfloat16)
        for copy in copies:
            copy.wait_send()

    for role in range(n_ctx):

        @pl.when(ctx == role)
        def _():
            exchange(role)

    @pl.when(ten == ctx)
    def _():
        for k in range(1, n_ten):
            skip_copy(k).wait_send()

    def finish_along(h, k):
        to, piece = along(h, k)

        @pl.when(to != ctx)
        def _():
            remote(piece, to).wait_send()

    for h in range(PARTS):
        for k in range(1, n_ten):
            across(h, k).wait_send()
        for k in range(n_ten):
            finish_along(h, k)
    for h in range(PARTS):
        for k in range(1, n_ten):
            gather_copy(h, k).wait_send()


def body(outer_gate, inner_gate, value_path, long_filter, skip_scale, out_weight):
    n_ctx = lax.axis_size("context")
    n_ten = lax.axis_size("tensor")
    positions, width = inner_gate.shape
    sub = width // n_ctx
    length = n_ctx * positions
    columns = out_weight.shape[1] // n_ten
    if n_ctx != 4 or n_ctx != n_ten or sub % (PARTS * 128) or length % BLOCK or columns % TILE or positions % 16 or length > 1024:
        return body_plain(outer_gate, inner_gate, value_path, long_filter, skip_scale, out_weight)
    tables = [jnp.asarray(t) for t in blocked_tables(length)]
    bf16, f32 = jnp.bfloat16, jnp.float32
    part = sub // PARTS
    dma = pltpu.SemaphoreType.DMA
    vmem = pl.BlockSpec(memory_space=pltpu.VMEM)
    hbm = pl.BlockSpec(memory_space=pl.ANY)
    return pl.pallas_call(
        functools.partial(fused, n_ctx, n_ten),
        out_shape=jax.ShapeDtypeStruct((positions, columns), bf16),
        in_specs=[vmem] * 5 + [hbm] * 5,
        out_specs=vmem,
        scratch_shapes=[
            pltpu.VMEM((out_weight.shape[0], columns), bf16),
            pltpu.VMEM((2 * length, length), bf16),
            pltpu.VMEM((2 * length, length), bf16),
            pltpu.VMEM((length, 2 * length), bf16),
            pltpu.VMEM((length, 2 * length), bf16),
            pltpu.VMEM((3, positions, width), bf16),
            pltpu.VMEM((PARTS, n_ten, 3, positions, part), bf16),
            pltpu.VMEM((PARTS, 3, length, part), bf16),
            pltpu.VMEM((8, width), f32),
            pltpu.VMEM((8, sub), f32),
            pltpu.VMEM((length, part), f32),
            pltpu.VMEM((length, n_ten * sub), bf16),
            pltpu.VMEM((n_ctx, positions, columns), bf16),
            pltpu.VMEM((n_ctx, positions, columns), bf16),
            pltpu.VMEM((positions, columns), f32),
            pltpu.VMEM((positions, columns), f32),
            dma((5,)),
            dma((PARTS, n_ten)), dma((PARTS, n_ten)),
            dma((PARTS, n_ten)), dma((PARTS, n_ctx)),
            dma((n_ten,)), dma((1,)),
            dma((PARTS, n_ten)), dma((PARTS, n_ten)),
            dma((n_ctx,)), dma((n_ctx,)),
        ],
        compiler_params=pltpu.CompilerParams(
            collective_id=0, has_side_effects=True, vmem_limit_bytes=56 * 1024 * 1024
        ),
    )(outer_gate, inner_gate, value_path, long_filter, skip_scale[None, :], out_weight, *tables)


def solution(mesh):
    placed = (
        P(("groups", "context"), "tensor"),
        P(("groups", "context"), "tensor"),
        P(("groups", "context"), "tensor"),
        P("context", "tensor"),
        P("tensor"),
        P("context", None),
    )
    return jax.shard_map(
        body,
        mesh=mesh,
        in_specs=placed,
        out_specs=P(("groups", "context"), "tensor"),
        check_vma=False,
    )
```
